32 devices in a mesh: grp: 2 (over x), tm: 16 (over z, y, core).
Axes of the slice: x: 2, y: 2, z: 4, core: 2. Of those that a mesh axis runs over, the one named last changes fastest.
Arguments:
- observations: bfloat16 [65536, 1024], P(('grp', 'tm')), parts along dimension 0, may hold values from -0.1875 to 0.1875
- counts: int32 [32], P(('grp', 'tm')), parts along dimension 0, may hold values from 1 to 2048, 10922 in all
- prior: float32 [32, 1024], P(('grp', 'tm')), parts along dimension 0, may hold values from 0.5 to 4
Outputs:
- factors: float32 [32, 1024, 1024], P(('grp', 'tm')), parts along dimension 0
The draws below stay inside these ranges and needn't reach their ends.
There are 2 independent parts, one for each index of `grp`. The reference program is written for one: setup_inputs(seed, part) draws one part's arguments, and reference() takes and returns one part's arrays. A program takes and returns all parts, laid end to end along the dimension named above; each array names one. Nothing has to cross between parts.
Inputs may be any that keep to these rules, and one draw needn't show every extreme that they name: `counts`: some step has exactly 2048 live rows in every draw.
All inputs are finite; a program needn't handle non-finite values. No bound on the sum of `counts` on one device may be relied on, other than what follows from the above.
Results may differ from the reference program's by a relative error of at most 0.0003.
Values sent between devices are 32-bit elements; how exact they have to be, the bound alone decides.
A program may use at most 64 MiB of HBM per device.

```python
import math
import jax
import jax.numpy as jnp
import numpy as np
from jax import lax

S = 1024
CAP = 2048
STEPS = 16


def level_of(rng, shape, split, low, top_value):
    level = 1.0
    for dim, shards_of in split:
        steps = jax.random.uniform(jax.random.fold_in(jax.random.fold_in(rng, 6), dim), (shards_of,), jnp.float32, low / len(split), top_value / len(split))
        level = level * jnp.repeat(jnp.exp(steps), shape[dim] // shards_of).reshape((-1,) + (1,) * (len(shape) - 1 - dim))
    return level


def profile(number_of, total, reach, slope):
    weights = [(1 << 20) // math.isqrt(rank ** slope) + 1 for rank in range(2, number_of + 1)]
    rest, given = total - reach - (number_of - 1), [1] * (number_of - 1)
    while rest > 0:
        free = [i for i in range(number_of - 1) if given[i] < reach]
        mass, budget = sum([weights[i] for i in free]), rest
        for i in free:
            more = min(reach - given[i], max(1, budget * weights[i] // mass), rest)
            given[i] = given[i] + more
            rest = rest - more
    return np.array([reach] + given)


def uneven_parts(own_key, number_of, total, reach, lean):
    if number_of == 2:
        one = jax.random.randint(own_key, (), max(1, total - reach), min(reach, total - 1) + 1)
        return jnp.stack([one, total - one])
    sizes = jnp.asarray(profile(number_of, total, reach, lean), jnp.int32)
    twos = (number_of - 1) // 2
    donor, sink = sizes[1:1 + 2 * twos:2], sizes[2:2 + 2 * twos:2]
    slack = jnp.minimum(donor - 1, reach - sink)
    passed = jax.random.randint(jax.random.fold_in(own_key, 1), (twos,), 0, 1 << 20) % (slack + 1)
    sizes = sizes.at[1:1 + 2 * twos:2].set(donor - passed).at[2:2 + 2 * twos:2].set(sink + passed)
    return sizes[jax.random.permutation(jax.random.fold_in(own_key, 2), number_of)]


def scatter_about(rng, dims, width, reach, split=(), kind=jnp.bfloat16):
    result = width * jax.random.normal(rng, dims, jnp.float32)
    if split:
        result = result * level_of(rng, dims, split, -0.22, 0.18)
    return jnp.clip(result, -reach, reach).astype(kind)


def setup_inputs(seed: int = 0, part: int = 0) -> dict:
    seeds = jax.random.split(jax.random.key(seed), 4)
    own_keys = jax.random.split(jax.random.fold_in(seeds[3], part), 4)
    return {
        "observations": scatter_about(own_keys[0], (STEPS * CAP, S), S ** -0.5, 0.1875, ((0, 16),)),
        "counts": uneven_parts(own_keys[1], STEPS, STEPS * CAP // 3, CAP, 2).astype(jnp.int32),
        "prior": jnp.clip(jnp.exp(math.log(4.0) - 2.0794415 * jax.random.uniform(own_keys[2], (STEPS, S), jnp.float32) ** level_of(own_keys[2], (STEPS, S), ((0, 16),), -0.2, 0.2)), 0.5, 4.0),
    }


def masked_gram(observed, live_count, prior_step):
    capacity = observed.shape[0]
    row_index = jnp.arange(capacity, dtype=jnp.int32)
    widened = jnp.where((row_index < live_count)[:, None], observed.astype(jnp.float32), jnp.float32(0.0))
    gram_matrix = jnp.dot(widened.T.astype(jnp.float32), widened.astype(jnp.float32), precision=lax.Precision.HIGHEST, preferred_element_type=jnp.float32)
    return gram_matrix + jnp.diag(prior_step)

def reference(observations, counts, prior):
    stacked = observations.reshape(STEPS, CAP, S)
    grams = lax.map(lambda item: masked_gram(item[0], item[1], item[2]), (stacked, counts, prior))
    zeroed = jnp.zeros_like(grams)
    level_one = grams + jnp.concatenate([zeroed[:1], grams[:-1]], 0)
    level_two = level_one + jnp.concatenate([zeroed[:2], level_one[:-2]], 0)
    lower_factor = jnp.linalg.cholesky(level_two)
    return jnp.transpose(lower_factor, (0, 2, 1))
```

```python
import jax
import jax.numpy as jnp
from jax import lax
from jax.experimental import pallas as pl
from jax.experimental.pallas import tpu as pltpu
from jax.sharding import PartitionSpec as P


def from_behind(block, axis, distance):
    devices = range(lax.axis_size(axis))
    route = [(i - distance, i) for i in devices if i - distance in devices]
    return lax.ppermute(block, axis, route)


def row_gram(block_rows):
    return lax.dot_general(
        block_rows, block_rows, (((0,), (0,)), ((), ())), preferred_element_type=jnp.float32
    )


def tn(a, b):
    return lax.dot_general(a, b, (((0,), (0,)), ((), ())), preferred_element_type=jnp.float32)

def halves(x):
    hi = x.astype(jnp.bfloat16)
    return hi, (x - hi.astype(jnp.float32)).astype(jnp.bfloat16)

def spread(x):
    return jnp.broadcast_to(x, (8, 128))

def factor_rows(block):
    rows = [block[8 * t:8 * t + 8, :] for t in range(8)]
    sub = lax.broadcasted_iota(jnp.int32, (8, 128), 0)
    done = []
    for s in range(8):
        cols = {t: [spread(rows[t][:, 8 * s + m:8 * s + m + 1]) for m in range(8)] for t in range(s, 8)}
        e = [[spread(cols[s][m][q:q + 1, :]) if q >= m else None for m in range(8)] for q in range(8)]
        r = [spread(rows[s][q:q + 1, :]) for q in range(8)]
        for i in range(8):
            inv = lax.rsqrt(e[i][i])
            low = [e[m][i] * inv if m > i else None for m in range(8)]
            r[i] = r[i] * inv
            for m in range(i + 1, 8):
                for q in range(i + 1, m + 1):
                    e[m][q] = e[m][q] - low[m] * low[q]
                r[m] = r[m] - low[m] * r[i]
            for t in range(s + 1, 8):
                cols[t][i] = cols[t][i] * inv
                for m in range(i + 1, 8):
                    cols[t][m] = cols[t][m] - low[m] * cols[t][i]
                rows[t] = rows[t] - cols[t][i] * r[i]
        out = r[7]
        for q in range(7):
            out = jnp.where(sub == q, r[q], out)
        done.append(out)
    return jnp.concatenate(done, 0)

def cholesky_kernel(w_ref, out_ref, s1, s2):
    n = w_ref.shape[0]
    lane = lax.broadcasted_iota(jnp.int32, (64, 128), 1)
    sub = lax.broadcasted_iota(jnp.int32, (64, 128), 0)
    unit = jnp.where(lane - 64 == sub, 1.0, 0.0).astype(jnp.float32)
    for k in range(n // 128):
        c0 = 128 * k
        panel = w_ref[c0:c0 + 128, c0:]
        if k:
            panel = panel - tn(s1[:384 * k, c0:c0 + 128], s2[:384 * k, c0:])
            out_ref[c0:c0 + 128, :c0] = jnp.zeros((128, c0), jnp.float32)
        for h in range(2):
            p = panel[64 * h:64 * h + 64]
            if h:
                b0 = 384 * k
                p = p - tn(s1[b0:b0 + 192, c0:c0 + 128], s2[b0:b0 + 192, c0:])[64:]
            a = p[:, :128]
            if h:
                a = pltpu.roll(a, 64, 1)
            f = factor_rows(jnp.where(lane < 64, a, unit))
            g = jnp.where(lane < 64, pltpu.roll(f, 64, 1), f)
            ghi, glo = halves(g)
            phi, plo = halves(p)
            both = jnp.dot(jnp.concatenate([ghi, glo], 0), jnp.concatenate([phi, plo], 0), preferred_element_type=jnp.float32)
            r = both[:64] + both[64:]
            r0 = c0 + 64 * h
            head = jnp.where(lane >= sub + 64 * h, r[:, :128], 0.0)
            r = jnp.concatenate([head, r[:, 128:]], 1) if c0 + 128 < n else head
            out_ref[r0:r0 + 64, c0:] = r
            hi, lo = halves(r)
            b = 384 * k + 192 * h
            s1[b:b + 64, c0:] = hi
            s1[b + 64:b + 128, c0:] = hi
            s1[b + 128:b + 192, c0:] = lo
            s2[b:b + 64, c0:] = hi
            s2[b + 64:b + 128, c0:] = lo
            s2[b + 128:b + 192, c0:] = hi

def cholesky(w):
    n = w.shape[0]
    return pl.pallas_call(
        cholesky_kernel,
        out_shape=jax.ShapeDtypeStruct((n, n), jnp.float32),
        in_specs=[pl.BlockSpec(memory_space=pltpu.VMEM)],
        out_specs=pl.BlockSpec(memory_space=pltpu.VMEM),
        scratch_shapes=[pltpu.VMEM((3 * n, n), jnp.bfloat16), pltpu.VMEM((3 * n, n), jnp.bfloat16)],
        compiler_params=pltpu.CompilerParams(vmem_limit_bytes=48 << 20),
    )(w)


def body(observations, counts, prior):
    capacity, columns = observations.shape
    live_count = counts[0]
    row_index = lax.broadcasted_iota(jnp.int32, (capacity, 1), 0)
    masked = jnp.where(row_index < live_count, observations, jnp.zeros_like(observations))
    gram_matrix = row_gram(masked)
    gram_matrix = gram_matrix + jnp.diag(prior[0])
    level_one = gram_matrix + from_behind(gram_matrix, "tm", 1)
    level_two = level_one + from_behind(level_one, "tm", 2)
    upper_factor = cholesky(level_two)
    return upper_factor[None]


def solution(mesh):
    placed = (P(("grp", "tm"), None), P(("grp", "tm")), P(("grp", "tm"), None))
    return jax.shard_map(
        body, mesh=mesh, in_specs=placed, out_specs=P(("grp", "tm"), None, None), check_vma=False
    )
```

```python
import functools
import jax
import jax.numpy as jnp
from jax import lax
from jax.experimental import pallas as pl
from jax.experimental.pallas import tpu as pltpu
from jax.sharding import PartitionSpec as P


def tn(a, b):
    return lax.dot_general(a, b, (((0,), (0,)), ((), ())), preferred_element_type=jnp.float32)

def halves(x):
    hi = x.astype(jnp.bfloat16)
    return hi, (x - hi.astype(jnp.float32)).astype(jnp.bfloat16)

def spread(x):
    return jnp.broadcast_to(x, (8, 128))

def factor_rows(block):
    rows = [block[8 * t:8 * t + 8, :] for t in range(8)]
    sub = lax.broadcasted_iota(jnp.int32, (8, 128), 0)
    done = []
    for s in range(8):
        cols = {t: [spread(rows[t][:, 8 * s + m:8 * s + m + 1]) for m in range(8)] for t in range(s, 8)}
        e = [[spread(cols[s][m][q:q + 1, :]) if q >= m else None for m in range(8)] for q in range(8)]
        r = [spread(rows[s][q:q + 1, :]) for q in range(8)]
        for i in range(8):
            inv = lax.rsqrt(e[i][i])
            low = [e[m][i] * inv if m > i else None for m in range(8)]
            r[i] = r[i] * inv
            for m in range(i + 1, 8):
                for q in range(i + 1, m + 1):
                    e[m][q] = e[m][q] - low[m] * low[q]
                r[m] = r[m] - low[m] * r[i]
            for t in range(s + 1, 8):
                cols[t][i] = cols[t][i] * inv
                for m in range(i + 1, 8):
                    cols[t][m] = cols[t][m] - low[m] * cols[t][i]
                rows[t] = rows[t] - cols[t][i] * r[i]
        out = r[7]
        for q in range(7):
            out = jnp.where(sub == q, r[q], out)
        done.append(out)
    return jnp.concatenate(done, 0)


def window_kernel(steps, h_ref, count_ref, prior_ref, out_ref, gram, pair, near, behind, far, s1, s2,
                  send_gram, send_pair, send_on, got_near, got_behind, got_far):
    n = out_ref.shape[0]
    panels = n // 128
    t = lax.axis_index("tm")
    odd = lax.rem(t, 2) == 1
    even = jnp.logical_not(odd)

    def cut(ref, k):
        return ref.at[pl.ds(128 * k, 128), pl.ds(128 * k, n - 128 * k)]

    def copy(k, src, dst, send, recv, target):
        return pltpu.make_async_remote_copy(
            src_ref=cut(src, k), dst_ref=cut(dst, k), send_sem=send.at[k], recv_sem=recv.at[k],
            device_id={"tm": target}, device_id_type=pl.DeviceIdType.MESH)

    def gram_to_pair(k):
        return copy(k, gram, near, send_gram, got_near, t + 1)

    def gram_ahead(k):
        return copy(k, gram, far, send_gram, got_far, t + 3)

    def pair_ahead(k):
        return copy(k, pair, behind, send_pair, got_behind, t + 2)

    def pass_on(k):
        return copy(k, behind, behind, send_on, got_behind, t - 1)

    barrier = pltpu.get_barrier_semaphore()

    def greet(target):
        pl.semaphore_signal(barrier, inc=1, device_id={"tm": target}, device_id_type=pl.DeviceIdType.MESH)

    @pl.when(odd)
    def _():
        greet(t - 1)

        @pl.when(t >= 2)
        def _():
            greet(t - 2)

        @pl.when(t + 3 < steps)
        def _():
            pl.semaphore_wait(barrier, 3)

        @pl.when(t + 3 == steps)
        def _():
            pl.semaphore_wait(barrier, 2)

        @pl.when(t + 1 == steps)
        def _():
            pl.semaphore_wait(barrier, 1)

    @pl.when(even)
    def _():
        greet(t + 1)

        @pl.when(t >= 3)
        def _():
            greet(t - 3)

        pl.semaphore_wait(barrier, 1)

    count = count_ref[0]
    live = lax.broadcasted_iota(jnp.int32, (h_ref.shape[0], 128), 0) < count
    eye = lax.broadcasted_iota(jnp.int32, (128, 128), 0) == lax.broadcasted_iota(jnp.int32, (128, 128), 1)
    def add_pair(k):
        @pl.when(odd)
        def _():
            at = (slice(128 * k, 128 * k + 128), slice(128 * k, n))
            gram_to_pair(k).wait_recv()
            pair[at] = gram[at] + near[at]

            @pl.when(t + 2 < steps)
            def _():
                pair_ahead(k).start()

    for k in range(panels):
        c0 = 128 * k
        rows = h_ref[:, c0:c0 + 128]
        rows = jnp.where(live, rows, jnp.zeros_like(rows))
        g = tn(rows, h_ref[:, c0:])
        lead = g[:, :128] + jnp.where(eye, prior_ref[:, c0:c0 + 128], 0.0)
        gram[c0:c0 + 128, c0:c0 + 128] = lead
        if k + 1 < panels:
            gram[c0:c0 + 128, c0 + 128:] = g[:, 128:]

        @pl.when(even)
        def _():
            gram_to_pair(k).start()

        @pl.when(odd & (t + 3 < steps))
        def _():
            gram_ahead(k).start()

        if k:
            add_pair(k - 1)

    add_pair(panels - 1)

    lane = lax.broadcasted_iota(jnp.int32, (64, 128), 1)
    sub = lax.broadcasted_iota(jnp.int32, (64, 128), 0)
    unit = jnp.where(lane - 64 == sub, 1.0, 0.0).astype(jnp.float32)
    for k in range(panels):
        c0 = 128 * k
        at = (slice(c0, c0 + 128), slice(c0, n))

        @pl.when(t >= 2)
        def _():
            pair_ahead(k).wait_recv()

        @pl.when(odd & (t >= 2))
        def _():
            pass_on(k).start()
            out_ref[at] = pair[at] + behind[at]

        @pl.when(odd & (t < 2))
        def _():
            out_ref[at] = pair[at]

        @pl.when(even & (t < 2))
        def _():
            out_ref[at] = gram[at]

        @pl.when(even & (t == 2))
        def _():
            out_ref[at] = gram[at] + behind[at]

        @pl.when(even & (t >= 3))
        def _():
            gram_ahead(k).wait_recv()
            out_ref[at] = gram[at] + behind[at] + far[at]

        panel = out_ref[at]
        if k:
            panel = panel - tn(s1[:384 * k, c0:c0 + 128], s2[:384 * k, c0:])
            out_ref[c0:c0 + 128, :c0] = jnp.zeros((128, c0), jnp.float32)
        for h in range(2):
            p = panel[64 * h:64 * h + 64]
            if h:
                b0 = 384 * k
                p = p - tn(s1[b0:b0 + 192, c0:c0 + 128], s2[b0:b0 + 192, c0:])[64:]
            a = p[:, :128]
            if h:
                a = pltpu.roll(a, 64, 1)
            f = factor_rows(jnp.where(lane < 64, a, unit))
            g = jnp.where(lane < 64, pltpu.roll(f, 64, 1), f)
            ghi, glo = halves(g)
            phi, plo = halves(p)
            both = jnp.dot(jnp.concatenate([ghi, glo], 0), jnp.concatenate([phi, plo], 0), preferred_element_type=jnp.float32)
            r = both[:64] + both[64:]
            r0 = c0 + 64 * h
            head = jnp.where(lane >= sub + 64 * h, r[:, :128], 0.0)
            r = jnp.concatenate([head, r[:, 128:]], 1) if c0 + 128 < n else head
            out_ref[r0:r0 + 64, c0:] = r
            hi, lo = halves(r)
            b = 384 * k + 192 * h
            s1[b:b + 64, c0:] = hi
            s1[b + 64:b + 128, c0:] = hi
            s1[b + 128:b + 192, c0:] = lo
            s2[b:b + 64, c0:] = hi
            s2[b + 64:b + 128, c0:] = lo
            s2[b + 128:b + 192, c0:] = hi

    for k in range(panels):
        @pl.when(even)
        def _():
            gram_to_pair(k).wait_send()

        @pl.when(odd & (t + 3 < steps))
        def _():
            gram_ahead(k).wait_send()

        @pl.when(odd & (t + 2 < steps))
        def _():
            pair_ahead(k).wait_send()

        @pl.when(odd & (t >= 2))
        def _():
            pass_on(k).wait_send()


def body(observations, counts, prior):
    n = observations.shape[1]
    panels = n // 128
    full = pltpu.VMEM((n, n), jnp.float32)
    factor = pl.pallas_call(
        functools.partial(window_kernel, lax.axis_size("tm")),
        out_shape=jax.ShapeDtypeStruct((n, n), jnp.float32),
        in_specs=[pl.BlockSpec(memory_space=pltpu.VMEM), pl.BlockSpec(memory_space=pltpu.SMEM),
                  pl.BlockSpec(memory_space=pltpu.VMEM)],
        out_specs=pl.BlockSpec(memory_space=pltpu.VMEM),
        scratch_shapes=[full] * 5 + [pltpu.VMEM((3 * n, n), jnp.bfloat16)] * 2
        + [pltpu.SemaphoreType.DMA((panels,))] * 6,
        compiler_params=pltpu.CompilerParams(
            collective_id=0, has_side_effects=True, vmem_limit_bytes=56 << 20),
    )(observations, counts, prior)
    return factor[None]


def solution(mesh):
    placed = (P(("grp", "tm"), None), P(("grp", "tm")), P(("grp", "tm"), None))
    return jax.shard_map(
        body, mesh=mesh, in_specs=placed, out_specs=P(("grp", "tm"), None, None), check_vma=False
    )
```

```python
import functools
import jax
import jax.numpy as jnp
from jax import lax
from jax.experimental import pallas as pl
from jax.experimental.pallas import tpu as pltpu
from jax.sharding import PartitionSpec as P


def tn(a, b):
    return lax.dot_general(a, b, (((0,), (0,)), ((), ())), preferred_element_type=jnp.float32)

def halves(x):
    hi = x.astype(jnp.bfloat16)
    return hi, (x - hi.astype(jnp.float32)).astype(jnp.bfloat16)

def spread(x):
    return jnp.broadcast_to(x, (8, 128))

def factor_rows(block):
    rows = [block[8 * t:8 * t + 8, :] for t in range(8)]
    sub = lax.broadcasted_iota(jnp.int32, (8, 128), 0)
    done = []
    for s in range(8):
        cols = {t: [spread(rows[t][:, 8 * s + m:8 * s + m + 1]) for m in range(8)] for t in range(s, 8)}
        e = [[spread(cols[s][m][q:q + 1, :]) if q >= m else None for m in range(8)] for q in range(8)]
        r = [spread(rows[s][q:q + 1, :]) for q in range(8)]
        for i in range(8):
            inv = lax.rsqrt(e[i][i])
            low = [e[m][i] * inv if m > i else None for m in range(8)]
            r[i] = r[i] * inv
            for m in range(i + 1, 8):
                for q in range(i + 1, m + 1):
                    e[m][q] = e[m][q] - low[m] * low[q]
                r[m] = r[m] - low[m] * r[i]
            for t in range(s + 1, 8):
                cols[t][i] = cols[t][i] * inv
                for m in range(i + 1, 8):
                    cols[t][m] = cols[t][m] - low[m] * cols[t][i]
                rows[t] = rows[t] - cols[t][i] * r[i]
        out = r[7]
        for q in range(7):
            out = jnp.where(sub == q, r[q], out)
        done.append(out)
    return jnp.concatenate(done, 0)


def window_kernel(steps, h_ref, count_ref, prior_ref, out_ref, gram, pair, near, behind, far, relay, s1, s2,
                  send_gram, send_pair, send_on, got_near, got_behind, got_far,
                  send_off, got_relay):
    n = out_ref.shape[0]
    panels = n // 128
    t = lax.axis_index("tm")
    odd = lax.rem(t, 2) == 1
    even = jnp.logical_not(odd)

    def cut(ref, k):
        return ref.at[pl.ds(128 * k, 128), pl.ds(128 * k, n - 128 * k)]

    def copy(k, src, dst, send, recv, target):
        return pltpu.make_async_remote_copy(
            src_ref=cut(src, k), dst_ref=cut(dst, k), send_sem=send.at[k], recv_sem=recv.at[k],
            device_id={"tm": target}, device_id_type=pl.DeviceIdType.MESH)

    def gram_to_pair(k):
        return copy(k, gram, near, send_gram, got_near, t + 1)

    def gram_ahead(k):
        return copy(k, gram, far, send_gram, got_far, t + 3)

    def pair_ahead(k):
        return copy(k, pair, behind, send_pair, got_behind, t + 2)

    def pass_on(k):
        return copy(k, behind, behind, send_on, got_behind, t - 1)

    third = lax.rem(t, 4) == 3
    via = third & (t + 4 < steps)
    carries = third & (t >= 4)

    def relay_out(k):
        return copy(k, pair, relay, send_pair, got_relay, t + 4)

    def relay_on(k):
        return copy(k, relay, behind, send_off, got_behind, t - 2)

    barrier = pltpu.get_barrier_semaphore()

    def greet(target):
        pl.semaphore_signal(barrier, inc=1, device_id={"tm": target}, device_id_type=pl.DeviceIdType.MESH)

    @pl.when(odd)
    def _():
        greet(t - 1)

        @pl.when(t >= 2)
        def _():
            greet(t - 2)

        @pl.when(carries)
        def _():
            greet(t - 4)

        @pl.when((lax.rem(t, 4) == 1) & (t >= 5) & (t + 2 < steps))
        def _():
            greet(t + 2)

        targets = {}
        for v in range(1, steps, 2):
            number = 1 + (v + 2 < steps) + (v + 3 < steps)
            if v % 4 == 3:
                number += (v + 4 < steps) + (v >= 4)
            targets.setdefault(number, []).append(t == v)
        for number, cases in targets.items():
            @pl.when(functools.reduce(jnp.logical_or, cases))
            def _():
                pl.semaphore_wait(barrier, number)

    @pl.when(even)
    def _():
        greet(t + 1)

        @pl.when(t >= 3)
        def _():
            greet(t - 3)

        pl.semaphore_wait(barrier, 1)

    count = count_ref[0]
    live = lax.broadcasted_iota(jnp.int32, (h_ref.shape[0], 128), 0) < count
    eye = lax.broadcasted_iota(jnp.int32, (128, 128), 0) == lax.broadcasted_iota(jnp.int32, (128, 128), 1)
    def add_pair(k):
        @pl.when(odd)
        def _():
            at = (slice(128 * k, 128 * k + 128), slice(128 * k, n))
            gram_to_pair(k).wait_recv()
            pair[at] = gram[at] + near[at]

            if k % 2:
                @pl.when(via)
                def _():
                    relay_out(k).start()

                @pl.when(jnp.logical_not(via) & (t + 2 < steps))
                def _():
                    pair_ahead(k).start()
            else:
                @pl.when(t + 2 < steps)
                def _():
                    pair_ahead(k).start()

    for k in range(panels):
        c0 = 128 * k
        rows = h_ref[:, c0:c0 + 128]
        rows = jnp.where(live, rows, jnp.zeros_like(rows))
        g = tn(rows, h_ref[:, c0:])
        lead = g[:, :128] + jnp.where(eye, prior_ref[:, c0:c0 + 128], 0.0)
        gram[c0:c0 + 128, c0:c0 + 128] = lead
        if k + 1 < panels:
            gram[c0:c0 + 128, c0 + 128:] = g[:, 128:]

        @pl.when(even)
        def _():
            gram_to_pair(k).start()

        @pl.when(odd & (t + 3 < steps))
        def _():
            gram_ahead(k).start()

        if k:
            add_pair(k - 1)

    add_pair(panels - 1)

    lane = lax.broadcasted_iota(jnp.int32, (64, 128), 1)
    sub = lax.broadcasted_iota(jnp.int32, (64, 128), 0)
    unit = jnp.where(lane - 64 == sub, 1.0, 0.0).astype(jnp.float32)
    for k in range(panels):
        c0 = 128 * k
        at = (slice(c0, c0 + 128), slice(c0, n))

        if k % 2:
            @pl.when(carries)
            def _():
                relay_out(k).wait_recv()
                relay_on(k).start()

        @pl.when(t >= 2)
        def _():
            pair_ahead(k).wait_recv()

        @pl.when(odd & (t >= 2))
        def _():
            pass_on(k).start()
            out_ref[at] = pair[at] + behind[at]

        @pl.when(odd & (t < 2))
        def _():
            out_ref[at] = pair[at]

        @pl.when(even & (t < 2))
        def _():
            out_ref[at] = gram[at]

        @pl.when(even & (t == 2))
        def _():
            out_ref[at] = gram[at] + behind[at]

        @pl.when(even & (t >= 3))
        def _():
            gram_ahead(k).wait_recv()
            out_ref[at] = gram[at] + behind[at] + far[at]

        panel = out_ref[at]
        if k:
            panel = panel - tn(s1[:384 * k, c0:c0 + 128], s2[:384 * k, c0:])
            out_ref[c0:c0 + 128, :c0] = jnp.zeros((128, c0), jnp.float32)
        for h in range(2):
            p = panel[64 * h:64 * h + 64]
            if h:
                b0 = 384 * k
                p = p - tn(s1[b0:b0 + 192, c0:c0 + 128], s2[b0:b0 + 192, c0:])[64:]
            a = p[:, :128]
            if h:
                a = pltpu.roll(a, 64, 1)
            f = factor_rows(jnp.where(lane < 64, a, unit))
            g = jnp.where(lane < 64, pltpu.roll(f, 64, 1), f)
            ghi, glo = halves(g)
            phi, plo = halves(p)
            both = jnp.dot(jnp.concatenate([ghi, glo], 0), jnp.concatenate([phi, plo], 0), preferred_element_type=jnp.float32)
            r = both[:64] + both[64:]
            r0 = c0 + 64 * h
            head = jnp.where(lane >= sub + 64 * h, r[:, :128], 0.0)
            r = jnp.concatenate([head, r[:, 128:]], 1) if c0 + 128 < n else head
            out_ref[r0:r0 + 64, c0:] = r
            hi, lo = halves(r)
            b = 384 * k + 192 * h
            s1[b:b + 64, c0:] = hi
            s1[b + 64:b + 128, c0:] = hi
            s1[b + 128:b + 192, c0:] = lo
            s2[b:b + 64, c0:] = hi
            s2[b + 64:b + 128, c0:] = lo
            s2[b + 128:b + 192, c0:] = hi

    for k in range(panels):
        @pl.when(even)
        def _():
            gram_to_pair(k).wait_send()

        @pl.when(odd & (t + 3 < steps))
        def _():
            gram_ahead(k).wait_send()

        @pl.when(odd & (t + 2 < steps))
        def _():
            pair_ahead(k).wait_send()

        @pl.when(odd & (t >= 2))
        def _():
            pass_on(k).wait_send()

        if k % 2:
            @pl.when(carries)
            def _():
                relay_on(k).wait_send()


def body(observations, counts, prior):
    n = observations.shape[1]
    panels = n // 128
    full = pltpu.VMEM((n, n), jnp.float32)
    factor = pl.pallas_call(
        functools.partial(window_kernel, lax.axis_size("tm")),
        out_shape=jax.ShapeDtypeStruct((n, n), jnp.float32),
        in_specs=[pl.BlockSpec(memory_space=pltpu.VMEM), pl.BlockSpec(memory_space=pltpu.SMEM),
                  pl.BlockSpec(memory_space=pltpu.VMEM)],
        out_specs=pl.BlockSpec(memory_space=pltpu.VMEM),
        scratch_shapes=[full] * 6 + [pltpu.VMEM((3 * n, n), jnp.bfloat16)] * 2
        + [pltpu.SemaphoreType.DMA((panels,))] * 8,
        compiler_params=pltpu.CompilerParams(
            collective_id=0, has_side_effects=True, vmem_limit_bytes=56 << 20),
    )(observations, counts, prior)
    return factor[None]


def solution(mesh):
    placed = (P(("grp", "tm"), None), P(("grp", "tm")), P(("grp", "tm"), None))
    return jax.shard_map(
        body, mesh=mesh, in_specs=placed, out_specs=P(("grp", "tm"), None, None), check_vma=False
    )
```
